512 devices in a mesh: grid: 64 (over y_lo, z, core), member: 8 (over y_hi, x).
Axes of the slice: x: 4, y: 4 (y_hi: 2, y_lo: 2; y = y_hi * 2 + y_lo), z: 16, core: 2. Of those that a mesh axis runs over, the one named last changes fastest.
Arguments:
- states: bfloat16 [8, 65536, 1024], P('member', 'grid'), may hold values from -6 to 6
- weight: bfloat16 [1024, 100], replicated, may hold values from -0.1875 to 0.1875
- target: float32 [100, 65536], P(None, 'grid'), may hold values from -6 to 6
- area: float32 [65536], P('grid'), may hold values from 0.5 to 4.5
Outputs:
- loss: float32 [], replicated
- grad_states: bfloat16 [8, 65536, 1024], P('member', 'grid')
- grad_weight: float32 [1024, 100], replicated
The draws below stay inside these ranges and needn't reach their ends.
All inputs are finite; a program needn't handle non-finite values.
Results may differ from the reference program's by a relative error of at most 0.0049.
Values may be sent and summed in bfloat16 or wider, within the bound.
No kernel may reach another device: no remote copies, remote signals or barrier semaphores. Data moves between devices by JAX's collectives and lax.ppermute only.
A program may use at most 64 MiB of HBM per device.

```python
import jax
import jax.numpy as jnp
from jax import lax

D = 1024
V = 100
GRID = 65536
MEMBERS = 8


def draw_area(key, part):
    key = jax.random.fold_in(key, 7)
    place = jnp.arange(GRID).astype(jnp.float32)
    ramp = 1.0 + 2.0 * place / (GRID - 1)
    rough = jax.random.uniform(key, (GRID,), jnp.float32, 0.5, 1.5)
    return ramp * rough


def block_levels(own_key, extent, shards, smallest, top_value):
    gain, own = 1.0, jax.random.fold_in(own_key, 6)
    for axis_at, blocks in shards:
        steps = jnp.exp(jax.random.uniform(jax.random.fold_in(own, axis_at), (blocks,), jnp.float32, smallest / len(shards), top_value / len(shards)))
        gain = gain * jnp.repeat(steps, extent[axis_at] // blocks).reshape([-1 if axis == axis_at else 1 for axis in range(len(extent))])
    return gain


def gaussian(own_key, dims, width, most, cuts=(), dtype=jnp.bfloat16):
    array = jax.random.normal(own_key, dims, jnp.float32) * width
    if len(cuts) > 0:
        array = block_levels(own_key, dims, cuts, -0.22, 0.18) * array
    return jnp.clip(array, min=-most, max=most).astype(dtype)


def setup_inputs(seed: int = 0) -> dict:
    splits = jax.random.split(jax.random.key(seed), 5)
    return {
        "states": gaussian(splits[0], (MEMBERS, GRID, D), 1.0, 6.0, ((0, 8), (1, 64))),
        "weight": gaussian(splits[1], (D, V), D ** -0.5, 0.1875),
        "target": gaussian(splits[2], (V, GRID), 1.0, 6.0, ((1, 64),), jnp.float32),
        "area": draw_area(jax.random.fold_in(splits[4], 71), 0),
    }


EPS_SQ = 0.0001

def smooth_abs(t):
    return jnp.sqrt(t * t + EPS_SQ)

def smooth_sign(t):
    return t / jnp.sqrt(t * t + EPS_SQ)

def reference(states, weight, target, area):

    def project(h):
        return lax.dot_general(weight, h, (((0,), (1,)), ((), ())), preferred_element_type=jnp.float32)
    pred = lax.map(project, states)
    diff_t = pred - target[None]
    pairsum = jnp.zeros(pred.shape, jnp.float32)
    pairgrad = jnp.zeros(pred.shape, jnp.float32)
    for other in range(MEMBERS):
        delta = pred - pred[other][None]
        pairsum = pairsum + smooth_abs(delta)
        pairgrad = pairgrad + smooth_sign(delta)
    coef = 1.0 / (MEMBERS - 1)
    per = smooth_abs(diff_t) - 0.5 * coef * pairsum
    loss_sum = jnp.sum(area[None, None, :] * per)
    loss = loss_sum / (GRID * V * MEMBERS)
    dpred = (area[None, None, :] * (smooth_sign(diff_t) - coef * pairgrad)).astype(jnp.bfloat16)

    def back(dm):
        return lax.dot_general(dm, weight, (((0,), (1,)), ((), ())), preferred_element_type=jnp.float32).astype(jnp.bfloat16)
    grad_states = lax.map(back, dpred)

    def wgrad(pair):
        h, dm = pair
        return lax.dot_general(h, dm, (((0,), (1,)), ((), ())), preferred_element_type=jnp.float32)
    grad_weight = lax.optimization_barrier(jnp.sum(lax.map(wgrad, (states, dpred)), axis=0)) / GRID
    return (loss, grad_states, grad_weight)
```

```python
import jax
import jax.numpy as jnp
from jax import lax
from jax.sharding import Mesh, PartitionSpec as P

EPS_SQ = 0.0001
V = 100
VPAD = 128
MEMBER = ("y_hi", "x")
GRID = ("y_lo", "z", "core")
PLANE = ("y_lo", "core", "y_hi", "x")
WSCALE = 0.25
ZSCALE = 1.0 / 1024.0


def exchange(x, axes):
    return lax.all_to_all(x, axes, 0, 0, tiled=True)


def smooth_inverse(t):
    return lax.rsqrt(t * t + EPS_SQ)


def shards(states, weight, target, area):
    local_states = states[0]
    members = lax.axis_size(MEMBER)
    plane = lax.axis_size(PLANE)
    depth = lax.axis_size("z")
    points, width = local_states.shape
    grid_total = points * lax.axis_size(GRID)
    own = points // members
    coef = 1.0 / (members - 1)
    rank = lax.axis_index(MEMBER)
    pred = lax.dot_general(
        weight, local_states, (((0,), (1,)), ((), ())), preferred_element_type=jnp.float32
    )
    parts = pred.reshape(V, members, own).transpose(1, 0, 2)
    every = exchange(parts, MEMBER)
    goal = lax.dynamic_slice_in_dim(target, rank * own, own, 1)
    weights = lax.dynamic_slice_in_dim(area, rank * own, own, 0)
    diff = every - goal[None]
    inv = smooth_inverse(diff)
    sign = diff * inv
    size = (diff * diff + EPS_SQ) * inv
    signs, sizes = [], jnp.zeros((V, own), jnp.float32)
    for m in range(members):
        delta = every[m][None] - every
        inv = smooth_inverse(delta)
        signs.append(jnp.sum(delta * inv, axis=0))
        sizes = sizes + jnp.sum((delta * delta + EPS_SQ) * inv, axis=0)
    per = jnp.sum(size, axis=0) - 0.5 * coef * sizes
    loss = jnp.sum(weights[None] * per)
    dpart = (weights * (sign - coef * jnp.stack(signs))).astype(jnp.bfloat16)
    dpred = exchange(dpart, MEMBER).transpose(1, 0, 2).reshape(V, points)
    grad_local = lax.dot_general(
        dpred, weight, (((0,), (1,)), ((), ())), preferred_element_type=jnp.float32
    ).astype(jnp.bfloat16)
    wterm = lax.dot_general(
        dpred, local_states, (((1,), (0,)), ((), ())), preferred_element_type=jnp.float32
    )
    wterm = jnp.pad(wterm * WSCALE, ((0, VPAD - V), (0, 0)))
    groups = VPAD // 32
    chunks = wterm.reshape(groups, 32, width // 128, 128).transpose(0, 2, 1, 3)
    chunks = chunks.reshape(plane, 32, 128).astype(jnp.float16)
    scaled = loss * (1.0 / 65536.0)
    high = scaled.astype(jnp.float16)
    low = ((scaled - high.astype(jnp.float32)) * 1024.0).astype(jnp.float16)
    chunks = chunks.at[plane - 1, 31, 0].set(high)
    chunks = chunks.at[plane - 1, 31, 1].set(low)
    mine = jnp.sum(exchange(chunks, PLANE).astype(jnp.float32), axis=0)
    mine = (mine * (1.0 / 32.0)).astype(jnp.float16)
    ring = exchange(jnp.broadcast_to(mine[None], (depth, 32, 128)), "z")
    mine = jnp.sum(ring.astype(jnp.float32), axis=0)
    mine = (mine * (1.0 / 16.0)).astype(jnp.float16)
    whole = exchange(jnp.broadcast_to(mine[None], (plane, 32, 128)), PLANE)
    factor = 512.0 / WSCALE / grid_total
    table = whole.astype(jnp.float32)
    grads = table.reshape(groups, width // 128, 32, 128).transpose(0, 2, 1, 3)
    grads = grads.reshape(VPAD, width)[:V] * factor
    total = (table[plane - 1, 31, 0] + table[plane - 1, 31, 1] * (1.0 / 1024.0)) * (512.0 * 65536.0)
    return (total / (grid_total * V * members), grad_local[None], grads.T)


def solution(mesh):
    fine = Mesh(mesh.devices.reshape(2, 16, 2, 2, 4), GRID + MEMBER)
    in_specs = (P(MEMBER, GRID, None), P(), P(None, GRID), P(GRID))
    out_specs = (P(), P(MEMBER, GRID, None), P())
    return jax.shard_map(shards, mesh=fine, in_specs=in_specs, out_specs=out_specs, check_vma=False)
```

```python
import jax
import jax.numpy as jnp
from jax import lax
from jax.experimental import pallas as pl
from jax.experimental.pallas import tpu as pltpu
from jax.sharding import Mesh, PartitionSpec as P

EPS_SQ = 0.0001
V = 100
VPAD = 128
BLOCK = 128
ROWS = 32
MEMBER = ("y_hi", "x")
GRID = ("y_lo", "z", "core")
PLANE = ("y_lo", "core", "y_hi", "x")
WSCALE = 0.25
LSCALE = 1.0 / 512.0
VMEM = pl.BlockSpec(memory_space=pltpu.VMEM)
SMEM = pl.BlockSpec(memory_space=pltpu.SMEM)


def exchange(x, axes):
    return lax.all_to_all(x, axes, 0, 0, tiled=True)


def pair_kernel(rank, diff, area, dpart, loss):
    members = diff.shape[0]
    coef = 1.0 / (members - 1)
    floor = coef * 0.5 * members * EPS_SQ**0.5
    weights = area[pl.ds(rank[0], 1), :]
    total = jnp.zeros((1, BLOCK), jnp.float32)
    for low in range(0, V, 16):
        high = min(low + 16, V)
        own = [diff[m, low:high, :] for m in range(members)]
        signs = [None] * members
        direct, size = None, None
        for m in range(members):
            square = own[m] * own[m] + EPS_SQ
            inv = lax.rsqrt(square)
            direct = square * inv if direct is None else direct + square * inv
            signs[m] = own[m] * inv
        pulls = [None] * members
        for i in range(members):
            for j in range(i + 1, members):
                delta = own[i] - own[j]
                square = delta * delta + EPS_SQ
                inv = lax.rsqrt(square)
                sign = delta * inv
                size = square * inv if size is None else size + square * inv
                pulls[i] = sign if pulls[i] is None else pulls[i] + sign
                pulls[j] = -sign if pulls[j] is None else pulls[j] - sign
        for m in range(members):
            dpart[m, low:high, :] = (weights * (signs[m] - coef * pulls[m])).astype(jnp.bfloat16)
        per = weights * (direct - coef * size - floor)
        total = total + jnp.sum(per, axis=0, keepdims=True)
    loss[...] = total


def pairs(rank, diff, area):
    return pl.pallas_call(
        pair_kernel,
        out_shape=(
            jax.ShapeDtypeStruct(diff.shape, jnp.bfloat16),
            jax.ShapeDtypeStruct((1, BLOCK), jnp.float32),
        ),
        in_specs=[SMEM, VMEM, VMEM],
        out_specs=(VMEM, VMEM),
        compiler_params=pltpu.CompilerParams(vmem_limit_bytes=8 * 1024 * 1024),
    )(rank, diff, area)


def finish_kernel(factor, loss_factor, table, grads, loss):
    columns = grads.shape[1] // BLOCK
    for g in range(VPAD // ROWS):
        rows = min(ROWS, V - g * ROWS)
        for c in range(columns):
            grads[g * ROWS : g * ROWS + rows, c * BLOCK : (c + 1) * BLOCK] = (
                table[g * columns + c, :rows, :] * factor
            )
    last = table.shape[0] - 1
    lanes = table[last, ROWS - 2 : ROWS - 1, :] + table[last, ROWS - 1 : ROWS, :] * (1.0 / 1024.0)
    loss[0, 0] = jnp.sum(lanes) * loss_factor


def finish(table, factor, loss_factor, width):
    return pl.pallas_call(
        lambda *refs: finish_kernel(factor, loss_factor, *refs),
        out_shape=(
            jax.ShapeDtypeStruct((V, width), jnp.float32),
            jax.ShapeDtypeStruct((1, 1), jnp.float32),
        ),
        in_specs=[VMEM],
        out_specs=(pl.BlockSpec((V, width), lambda: (0, 0)), SMEM),
        compiler_params=pltpu.CompilerParams(vmem_limit_bytes=8 * 1024 * 1024),
    )(table)


def shards(states, weight, target, area):
    members = lax.axis_size(MEMBER)
    plane = lax.axis_size(PLANE)
    depth = lax.axis_size("z")
    points, width = states.shape[1:]
    grid_total = points * lax.axis_size(GRID)
    rank = lax.axis_index(MEMBER)
    local_states = states[0]
    pred = lax.dot_general(
        weight, local_states, (((0,), (1,)), ((), ())), preferred_element_type=jnp.float32
    )
    diff = (pred - target).astype(jnp.float16).reshape(V, members, BLOCK).transpose(1, 0, 2)
    every = exchange(diff, MEMBER).astype(jnp.float32)
    dpart, loss = pairs(rank[None], every, area.reshape(members, BLOCK))
    dpred = exchange(dpart, MEMBER).transpose(1, 0, 2).reshape(V, points)
    grad_local = lax.dot_general(
        dpred, weight, (((0,), (1,)), ((), ())), preferred_element_type=jnp.float32
    ).astype(jnp.bfloat16)
    wterm = lax.dot_general(
        dpred, local_states, (((1,), (0,)), ((), ())), preferred_element_type=jnp.float32
    )
    scaled = loss * LSCALE
    top = scaled.astype(jnp.float16)
    rest = ((scaled - top.astype(jnp.float32)) * 1024.0).astype(jnp.float16)
    tail = jnp.concatenate([jnp.zeros((VPAD - V - 2, BLOCK), jnp.float16), top, rest])
    groups, columns = VPAD // ROWS, width // BLOCK
    wterm = jnp.concatenate([(wterm * WSCALE).astype(jnp.float16), jnp.tile(tail, (1, columns))])
    chunks = wterm.reshape(groups, ROWS, columns, BLOCK).transpose(0, 2, 1, 3)
    chunks = chunks.reshape(plane, ROWS, BLOCK)
    mine = jnp.sum(exchange(chunks, PLANE).astype(jnp.float32), axis=0)
    mine = (mine * (1.0 / plane)).astype(jnp.float16)
    ring = exchange(jnp.broadcast_to(mine[None], (depth, ROWS, BLOCK)), "z")
    mine = jnp.sum(ring.astype(jnp.float32), axis=0)
    mine = (mine * (1.0 / depth)).astype(jnp.float16)
    whole = exchange(jnp.broadcast_to(mine[None], (plane, ROWS, BLOCK)), PLANE)
    devices = plane * depth
    grads, total = finish(
        whole.astype(jnp.float32),
        devices / WSCALE / grid_total,
        devices / LSCALE / (grid_total * V * members),
        width,
    )
    return (total[0, 0], grad_local[None], grads.T)


def solution(mesh):
    fine = Mesh(mesh.devices.reshape(2, 16, 2, 2, 4), GRID + MEMBER)
    in_specs = (P(MEMBER, GRID, None), P(), P(None, GRID), P(GRID))
    out_specs = (P(), P(MEMBER, GRID, None), P())
    return jax.shard_map(shards, mesh=fine, in_specs=in_specs, out_specs=out_specs, check_vma=False)
```

```python
import jax
import jax.numpy as jnp
from jax import lax
from jax.experimental import pallas as pl
from jax.experimental.pallas import tpu as pltpu
from jax.sharding import Mesh, PartitionSpec as P

EPS_SQ = 0.0001
V = 100
BLOCK = 128
GROUPS = 4
MEMBER = ("y_hi", "x")
GRID = ("y_lo", "z", "core")
PLANE = ("y_lo", "core", "y_hi", "x")
WSCALE = 0.25
LSCALE = 1.0 / 512.0
VMEM = pl.BlockSpec(memory_space=pltpu.VMEM)
SMEM = pl.BlockSpec(memory_space=pltpu.SMEM)


def exchange(x, axes):
    return lax.all_to_all(x, axes, 0, 0, tiled=True)


def project_kernel(states, weight, goal, diff):
    for low in range(0, states.shape[0], 2 * BLOCK):
        both = lax.dot_general(
            weight[...],
            states[low : low + 2 * BLOCK, :],
            (((1,), (1,)), ((), ())),
            preferred_element_type=jnp.float32,
        )
        for part in range(2):
            r = low // BLOCK + part
            diff[r] = both[:V, part * BLOCK : (part + 1) * BLOCK] - goal[r]


def project(states, weight, goal):
    return pl.pallas_call(
        project_kernel,
        out_shape=jax.ShapeDtypeStruct(goal.shape, jnp.float32),
        in_specs=[VMEM, VMEM, VMEM],
        out_specs=VMEM,
        compiler_params=pltpu.CompilerParams(vmem_limit_bytes=8 * 1024 * 1024),
    )(states, weight, goal)


def pair_kernel(rank, diff, area, dpart, loss):
    members = diff.shape[0]
    coef = 1.0 / (members - 1)
    floor = coef * 0.5 * members * EPS_SQ**0.5
    weights = area[pl.ds(rank[0], 1), :]
    total = jnp.zeros((1, BLOCK), jnp.float32)
    for low in range(0, V, 16):
        high = min(low + 16, V)
        own = [diff[m, low:high, :] for m in range(members)]
        signs = [None] * members
        direct, size = None, None
        for m in range(members):
            square = own[m] * own[m] + EPS_SQ
            inv = lax.rsqrt(square)
            direct = square * inv if direct is None else direct + square * inv
            signs[m] = own[m] * inv
        pulls = [None] * members
        for i in range(members):
            for j in range(i + 1, members):
                delta = own[i] - own[j]
                square = delta * delta + EPS_SQ
                inv = lax.rsqrt(square)
                sign = delta * inv
                size = square * inv if size is None else size + square * inv
                pulls[i] = sign if pulls[i] is None else pulls[i] + sign
                pulls[j] = -sign if pulls[j] is None else pulls[j] - sign
        for m in range(members):
            dpart[m, low:high, :] = (weights * (signs[m] - coef * pulls[m])).astype(jnp.bfloat16)
        per = weights * (direct - coef * size - floor)
        total = total + jnp.sum(per, axis=0, keepdims=True)
    loss[...] = total


def pairs(rank, diff, area):
    return pl.pallas_call(
        pair_kernel,
        out_shape=(
            jax.ShapeDtypeStruct(diff.shape, jnp.bfloat16),
            jax.ShapeDtypeStruct((1, BLOCK), jnp.float32),
        ),
        in_specs=[SMEM, VMEM, VMEM],
        out_specs=(VMEM, VMEM),
        compiler_params=pltpu.CompilerParams(vmem_limit_bytes=8 * 1024 * 1024),
    )(rank, diff, area)


def finish_kernel(factor, loss_factor, table, grads, loss):
    columns = grads.shape[1] // BLOCK
    for g in range(GROUPS):
        for c in range(columns):
            piece = table[g * columns + c] * factor
            lanes = slice(c * BLOCK, (c + 1) * BLOCK)
            grads[24 * g : 24 * (g + 1), lanes] = piece[:24]
            grads[V - GROUPS + g : V - GROUPS + g + 1, lanes] = piece[24:25]
    lanes = table[0, 25:26, :] + table[1, 25:26, :] * (1.0 / 1024.0)
    loss[0, 0] = jnp.sum(lanes) * loss_factor


def finish(table, factor, loss_factor, width):
    return pl.pallas_call(
        lambda *refs: finish_kernel(factor, loss_factor, *refs),
        out_shape=(
            jax.ShapeDtypeStruct((V, width), jnp.float32),
            jax.ShapeDtypeStruct((1, 1), jnp.float32),
        ),
        in_specs=[VMEM],
        out_specs=(pl.BlockSpec((V, width), lambda: (0, 0)), SMEM),
        compiler_params=pltpu.CompilerParams(vmem_limit_bytes=8 * 1024 * 1024),
    )(table)


def shards(states, weight, target, area):
    members = lax.axis_size(MEMBER)
    plane = lax.axis_size(PLANE)
    depth = lax.axis_size("z")
    points, width = states.shape[1:]
    grid_total = points * lax.axis_size(GRID)
    rank = lax.axis_index(MEMBER)
    local_states = states[0]
    columns = width // BLOCK
    goal = lax.optimization_barrier(target.reshape(V, members, BLOCK).transpose(1, 0, 2))
    diff = project(local_states, jnp.pad(weight.T, ((0, 28), (0, 0))), goal)
    diff, rank = lax.optimization_barrier((diff.astype(jnp.float16), rank[None]))
    every = exchange(diff, MEMBER).astype(jnp.float32)
    dpart, loss = pairs(rank, every, area.reshape(members, BLOCK))
    scaled = loss * LSCALE
    top = scaled.astype(jnp.float16)
    rest = ((scaled - top.astype(jnp.float32)) * 1024.0).astype(jnp.float16)
    spare = jnp.concatenate([top, rest])[None, None]
    spare = jnp.broadcast_to(spare, (GROUPS, columns // 2, 2, BLOCK))
    spare = spare.reshape(GROUPS, columns, 1, BLOCK)
    dpart, spare = lax.optimization_barrier((dpart, spare))
    dpred = exchange(dpart, MEMBER).transpose(1, 0, 2).reshape(V, points)
    grad_local = lax.dot_general(
        dpred, weight, (((0,), (1,)), ((), ())), preferred_element_type=jnp.float32
    ).astype(jnp.bfloat16)
    wterm = lax.dot_general(
        dpred, local_states, (((1,), (0,)), ((), ())), preferred_element_type=jnp.float32
    )
    wterm = (wterm * WSCALE).astype(jnp.float16)
    body = wterm[: V - GROUPS].reshape(GROUPS, 24, columns, BLOCK).transpose(0, 2, 1, 3)
    last = wterm[V - GROUPS :].reshape(GROUPS, columns, 1, BLOCK)
    chunks = jnp.concatenate([body, last, spare], axis=2).reshape(plane, 13, 2, BLOCK)
    mine = jnp.sum(exchange(chunks, PLANE).astype(jnp.float32), axis=0)
    mine = (mine * (1.0 / plane)).astype(jnp.float16)
    ring = exchange(jnp.broadcast_to(mine[None], (depth, 13, 2, BLOCK)), "z")
    mine = jnp.sum(ring.astype(jnp.float32), axis=0)
    mine = (mine * (1.0 / depth)).astype(jnp.float16)
    whole = exchange(jnp.broadcast_to(mine[None], (plane, 13, 2, BLOCK)), PLANE)
    whole = whole.reshape(plane, 26, BLOCK)
    devices = plane * depth
    grads, total = finish(
        whole.astype(jnp.float32),
        devices / WSCALE / grid_total,
        devices / LSCALE / (grid_total * V * members),
        width,
    )
    return (total[0, 0], grad_local[None], grads.T)


def solution(mesh):
    fine = Mesh(mesh.devices.reshape(2, 16, 2, 2, 4), GRID + MEMBER)
    in_specs = (P(MEMBER, GRID, None), P(), P(None, GRID), P(GRID))
    out_specs = (P(), P(MEMBER, GRID, None), P())
    return jax.shard_map(shards, mesh=fine, in_specs=in_specs, out_specs=out_specs, check_vma=False)
```

```python
import itertools

import jax
import jax.numpy as jnp
from jax import lax
from jax.experimental import pallas as pl
from jax.experimental.pallas import tpu as pltpu
from jax.sharding import Mesh, PartitionSpec as P

EPS_SQ = 0.0001
V = 100
BLOCK = 128
GROUPS = 4
MEMBER = ("y_hi", "x")
GRID = ("y_lo", "z", "core")
PLANE = ("y_hi", "y_lo", "x", "core")
MEMBER_FIRST = (1, 2)
PLANE_FIRST = (1, 0, 2, 0)
Z_FIRST = (8,)
WSCALE = 0.25
LSCALE = 1.0 / 512.0
VMEM = pl.BlockSpec(memory_space=pltpu.VMEM)
SMEM = pl.BlockSpec(memory_space=pltpu.SMEM)


def places(axes, first):
    sizes = [lax.axis_size(a) for a in axes]
    order = []
    for place in itertools.product(*map(range, sizes)):
        index = 0
        for step, begin, size in zip(place, first, sizes):
            index = index * size + (begin + step) % size
        order.append(index)
    return order


def exchange(x, axes, first):
    return lax.all_to_all(x, axes, 0, 0, axis_index_groups=[places(axes, first)], tiled=True)


def project_kernel(states, weight, goal, diff):
    for low in range(0, states.shape[0], 2 * BLOCK):
        both = lax.dot_general(
            weight[...],
            states[low : low + 2 * BLOCK, :],
            (((1,), (1,)), ((), ())),
            preferred_element_type=jnp.float32,
        )
        for part in range(2):
            r = low // BLOCK + part
            diff[r] = both[:V, part * BLOCK : (part + 1) * BLOCK] - goal[r]


def project(states, weight, goal):
    return pl.pallas_call(
        project_kernel,
        out_shape=jax.ShapeDtypeStruct(goal.shape, jnp.float32),
        in_specs=[VMEM, VMEM, VMEM],
        out_specs=VMEM,
        compiler_params=pltpu.CompilerParams(vmem_limit_bytes=8 * 1024 * 1024),
    )(states, weight, goal)


def pair_kernel(rank, diff, area, dpart, loss):
    members = diff.shape[0]
    coef = 1.0 / (members - 1)
    floor = coef * 0.5 * members * EPS_SQ**0.5
    weights = area[pl.ds(rank[0], 1), :]
    total = jnp.zeros((1, BLOCK), jnp.float32)
    for low in range(0, V, 16):
        high = min(low + 16, V)
        own = [diff[m, low:high, :] for m in range(members)]
        signs = [None] * members
        direct, size = None, None
        for m in range(members):
            square = own[m] * own[m] + EPS_SQ
            inv = lax.rsqrt(square)
            direct = square * inv if direct is None else direct + square * inv
            signs[m] = own[m] * inv
        pulls = [None] * members
        for i in range(members):
            for j in range(i + 1, members):
                delta = own[i] - own[j]
                square = delta * delta + EPS_SQ
                inv = lax.rsqrt(square)
                sign = delta * inv
                size = square * inv if size is None else size + square * inv
                pulls[i] = sign if pulls[i] is None else pulls[i] + sign
                pulls[j] = -sign if pulls[j] is None else pulls[j] - sign
        for m in range(members):
            dpart[m, low:high, :] = (weights * (signs[m] - coef * pulls[m])).astype(jnp.bfloat16)
        per = weights * (direct - coef * size - floor)
        total = total + jnp.sum(per, axis=0, keepdims=True)
    loss[...] = total


def pairs(rank, diff, area):
    return pl.pallas_call(
        pair_kernel,
        out_shape=(
            jax.ShapeDtypeStruct(diff.shape, jnp.bfloat16),
            jax.ShapeDtypeStruct((1, BLOCK), jnp.float32),
        ),
        in_specs=[SMEM, VMEM, VMEM],
        out_specs=(VMEM, VMEM),
        compiler_params=pltpu.CompilerParams(vmem_limit_bytes=8 * 1024 * 1024),
    )(rank, diff, area)


def finish_kernel(factor, loss_factor, table, grads, loss):
    columns = grads.shape[1] // BLOCK
    for g in range(GROUPS):
        for c in range(columns):
            piece = table[g * columns + c] * factor
            lanes = slice(c * BLOCK, (c + 1) * BLOCK)
            grads[24 * g : 24 * (g + 1), lanes] = piece[:24]
            grads[V - GROUPS + g : V - GROUPS + g + 1, lanes] = piece[24:25]
    lanes = table[0, 25:26, :] + table[1, 25:26, :] * (1.0 / 1024.0)
    loss[0, 0] = jnp.sum(lanes) * loss_factor


def finish(table, factor, loss_factor, width):
    return pl.pallas_call(
        lambda *refs: finish_kernel(factor, loss_factor, *refs),
        out_shape=(
            jax.ShapeDtypeStruct((V, width), jnp.float32),
            jax.ShapeDtypeStruct((1, 1), jnp.float32),
        ),
        in_specs=[VMEM],
        out_specs=(pl.BlockSpec((V, width), lambda: (0, 0)), SMEM),
        compiler_params=pltpu.CompilerParams(vmem_limit_bytes=8 * 1024 * 1024),
    )(table)


def shards(states, weight, target, area):
    members = lax.axis_size(MEMBER)
    plane = lax.axis_size(PLANE)
    depth = lax.axis_size("z")
    points, width = states.shape[1:]
    grid_total = points * lax.axis_size(GRID)
    rank = 0
    for axis, begin in zip(MEMBER, MEMBER_FIRST):
        size = lax.axis_size(axis)
        rank = rank * size + (lax.axis_index(axis) + size - begin) % size
    local_states = states[0]
    columns = width // BLOCK
    goal = lax.optimization_barrier(target.reshape(V, members, BLOCK).transpose(1, 0, 2))
    diff = project(local_states, jnp.pad(weight.T, ((0, 28), (0, 0))), goal)
    diff, rank = lax.optimization_barrier((diff.astype(jnp.float16), rank[None]))
    every = exchange(diff, MEMBER, MEMBER_FIRST).astype(jnp.float32)
    dpart, loss = pairs(rank, every, area.reshape(members, BLOCK))
    scaled = loss * LSCALE
    top = scaled.astype(jnp.float16)
    rest = ((scaled - top.astype(jnp.float32)) * 1024.0).astype(jnp.float16)
    spare = jnp.concatenate([top, rest])[None, None]
    spare = jnp.broadcast_to(spare, (GROUPS, columns // 2, 2, BLOCK))
    spare = spare.reshape(GROUPS, columns, 1, BLOCK)
    dpart, spare = lax.optimization_barrier((dpart, spare))
    dpred = exchange(dpart, MEMBER, MEMBER_FIRST).transpose(1, 0, 2).reshape(V, points)
    grad_local = lax.dot_general(
        dpred, weight, (((0,), (1,)), ((), ())), preferred_element_type=jnp.float32
    ).astype(jnp.bfloat16)
    wterm = lax.dot_general(
        dpred, local_states, (((1,), (0,)), ((), ())), preferred_element_type=jnp.float32
    )
    wterm = (wterm * WSCALE).astype(jnp.float16)
    body = wterm[: V - GROUPS].reshape(GROUPS, 24, columns, BLOCK).transpose(0, 2, 1, 3)
    last = wterm[V - GROUPS :].reshape(GROUPS, columns, 1, BLOCK)
    chunks = jnp.concatenate([body, last, spare], axis=2).reshape(plane, 13, 2, BLOCK)
    mine = jnp.sum(exchange(chunks, PLANE, PLANE_FIRST).astype(jnp.float32), axis=0)
    mine = (mine * (1.0 / plane)).astype(jnp.float16)
    ring = exchange(jnp.broadcast_to(mine[None], (depth, 13, 2, BLOCK)), ("z",), Z_FIRST)
    mine = jnp.sum(ring.astype(jnp.float32), axis=0)
    mine = (mine * (1.0 / depth)).astype(jnp.float16)
    whole = exchange(jnp.broadcast_to(mine[None], (plane, 13, 2, BLOCK)), PLANE, PLANE_FIRST)
    whole = whole.reshape(plane, 26, BLOCK)
    devices = plane * depth
    grads, total = finish(
        whole.astype(jnp.float32),
        devices / WSCALE / grid_total,
        devices / LSCALE / (grid_total * V * members),
        width,
    )
    return (total[0, 0], grad_local[None], grads.T)


def solution(mesh):
    fine = Mesh(mesh.devices.reshape(2, 16, 2, 2, 4), GRID + MEMBER)
    in_specs = (P(MEMBER, GRID, None), P(), P(None, GRID), P(GRID))
    out_specs = (P(), P(MEMBER, GRID, None), P())
    return jax.shard_map(shards, mesh=fine, in_specs=in_specs, out_specs=out_specs, check_vma=False)
```

```python
import itertools

import jax
import jax.numpy as jnp
from jax import lax
from jax.experimental import pallas as pl
from jax.experimental.pallas import tpu as pltpu
from jax.sharding import Mesh, PartitionSpec as P

EPS_SQ = 0.0001
V = 100
BLOCK = 128
GROUPS = 4
MEMBER = ("y_hi", "x")
GRID = ("y_lo", "z", "core")
PLANE = ("y_hi", "y_lo", "x", "core")
MEMBER_FIRST = (1, 2)
PLANE_FIRST = (1, 1, 2, 1)
Z_FIRST = (8,)
WSCALE = 0.25
LSCALE = 1.0 / 512.0
VMEM = pl.BlockSpec(memory_space=pltpu.VMEM)
SMEM = pl.BlockSpec(memory_space=pltpu.SMEM)


def places(axes, first):
    sizes = [lax.axis_size(a) for a in axes]
    order = []
    for place in itertools.product(*map(range, sizes)):
        index = 0
        for step, begin, size in zip(place, first, sizes):
            index = index * size + (begin + step) % size
        order.append(index)
    return order


def exchange(x, axes, first):
    return lax.all_to_all(x, axes, 0, 0, axis_index_groups=[places(axes, first)], tiled=True)


def project_kernel(states, weight, goal, diff):
    for low in range(0, states.shape[0], 2 * BLOCK):
        both = lax.dot_general(
            weight[...],
            states[low : low + 2 * BLOCK, :],
            (((1,), (1,)), ((), ())),
            preferred_element_type=jnp.float32,
        )
        for part in range(2):
            r = low // BLOCK + part
            diff[r] = both[:V, part * BLOCK : (part + 1) * BLOCK] - goal[r]


def project(states, weight, goal):
    return pl.pallas_call(
        project_kernel,
        out_shape=jax.ShapeDtypeStruct(goal.shape, jnp.float32),
        in_specs=[VMEM, VMEM, VMEM],
        out_specs=VMEM,
        compiler_params=pltpu.CompilerParams(vmem_limit_bytes=8 * 1024 * 1024),
    )(states, weight, goal)


def pair_kernel(rank, diff, area, dpart, loss):
    members = diff.shape[0]
    coef = 1.0 / (members - 1)
    floor = coef * 0.5 * members * EPS_SQ**0.5
    weights = area[pl.ds(rank[0], 1), :]
    total = jnp.zeros((1, BLOCK), jnp.float32)
    for low in range(0, V, 16):
        high = min(low + 16, V)
        own = [diff[m, low:high, :] for m in range(members)]
        signs = [None] * members
        direct, size = None, None
        for m in range(members):
            square = own[m] * own[m] + EPS_SQ
            inv = lax.rsqrt(square)
            direct = square * inv if direct is None else direct + square * inv
            signs[m] = own[m] * inv
        pulls = [None] * members
        for i in range(members):
            for j in range(i + 1, members):
                delta = own[i] - own[j]
                square = delta * delta + EPS_SQ
                inv = lax.rsqrt(square)
                sign = delta * inv
                size = square * inv if size is None else size + square * inv
                pulls[i] = sign if pulls[i] is None else pulls[i] + sign
                pulls[j] = -sign if pulls[j] is None else pulls[j] - sign
        for m in range(members):
            dpart[m, low:high, :] = (weights * (signs[m] - coef * pulls[m])).astype(jnp.bfloat16)
        per = weights * (direct - coef * size - floor)
        total = total + jnp.sum(per, axis=0, keepdims=True)
    loss[...] = total


def pairs(rank, diff, area):
    return pl.pallas_call(
        pair_kernel,
        out_shape=(
            jax.ShapeDtypeStruct(diff.shape, jnp.bfloat16),
            jax.ShapeDtypeStruct((1, BLOCK), jnp.float32),
        ),
        in_specs=[SMEM, VMEM, VMEM],
        out_specs=(VMEM, VMEM),
        compiler_params=pltpu.CompilerParams(vmem_limit_bytes=8 * 1024 * 1024),
    )(rank, diff, area)


def finish_kernel(factor, loss_factor, table, grads, loss):
    columns = grads.shape[1] // BLOCK
    for g in range(GROUPS):
        for c in range(columns):
            piece = table[g * columns + c] * factor
            lanes = slice(c * BLOCK, (c + 1) * BLOCK)
            grads[24 * g : 24 * (g + 1), lanes] = piece[:24]
            grads[V - GROUPS + g : V - GROUPS + g + 1, lanes] = piece[24:25]
    lanes = table[0, 25:26, :] + table[1, 25:26, :] * (1.0 / 1024.0)
    loss[0, 0] = jnp.sum(lanes) * loss_factor


def finish(table, factor, loss_factor, width):
    return pl.pallas_call(
        lambda *refs: finish_kernel(factor, loss_factor, *refs),
        out_shape=(
            jax.ShapeDtypeStruct((V, width), jnp.float32),
            jax.ShapeDtypeStruct((1, 1), jnp.float32),
        ),
        in_specs=[VMEM],
        out_specs=(pl.BlockSpec((V, width), lambda: (0, 0)), SMEM),
        compiler_params=pltpu.CompilerParams(vmem_limit_bytes=8 * 1024 * 1024),
    )(table)


def shards(states, weight, target, area):
    members = lax.axis_size(MEMBER)
    plane = lax.axis_size(PLANE)
    depth = lax.axis_size("z")
    points, width = states.shape[1:]
    grid_total = points * lax.axis_size(GRID)
    rank = 0
    for axis, begin in zip(MEMBER, MEMBER_FIRST):
        size = lax.axis_size(axis)
        rank = rank * size + (lax.axis_index(axis) + size - begin) % size
    local_states = states[0]
    columns = width // BLOCK
    goal = lax.optimization_barrier(target.reshape(V, members, BLOCK).transpose(1, 0, 2))
    diff = project(local_states, jnp.pad(weight.T, ((0, 28), (0, 0))), goal)
    diff, rank = lax.optimization_barrier((diff.astype(jnp.float16), rank[None]))
    every = exchange(diff, MEMBER, MEMBER_FIRST).astype(jnp.float32)
    dpart, loss = pairs(rank, every, area.reshape(members, BLOCK))
    scaled = loss * LSCALE
    top = scaled.astype(jnp.float16)
    rest = ((scaled - top.astype(jnp.float32)) * 1024.0).astype(jnp.float16)
    spare = jnp.concatenate([top, rest])[None, None]
    spare = jnp.broadcast_to(spare, (GROUPS, columns // 2, 2, BLOCK))
    spare = spare.reshape(GROUPS, columns, 1, BLOCK)
    dpart, spare = lax.optimization_barrier((dpart, spare))
    dpred = exchange(dpart, MEMBER, MEMBER_FIRST).transpose(1, 0, 2).reshape(V, points)
    grad_local = lax.dot_general(
        dpred, weight, (((0,), (1,)), ((), ())), preferred_element_type=jnp.float32
    ).astype(jnp.bfloat16)
    wterm = lax.dot_general(
        dpred, local_states, (((1,), (0,)), ((), ())), preferred_element_type=jnp.float32
    )
    wterm = (wterm * WSCALE).astype(jnp.float16)
    body = wterm[: V - GROUPS].reshape(GROUPS, 24, columns, BLOCK).transpose(0, 2, 1, 3)
    last = wterm[V - GROUPS :].reshape(GROUPS, columns, 1, BLOCK)
    chunks = jnp.concatenate([body, last, spare], axis=2).reshape(plane, 13, 2, BLOCK)
    mine = jnp.sum(exchange(chunks, PLANE, PLANE_FIRST).astype(jnp.float32), axis=0)
    mine = (mine * (1.0 / plane)).astype(jnp.float16)
    ring = exchange(jnp.broadcast_to(mine[None], (depth, 13, 2, BLOCK)), ("z",), Z_FIRST)
    mine = jnp.sum(ring.astype(jnp.float32), axis=0)
    mine = (mine * (1.0 / depth)).astype(jnp.float16)
    whole = exchange(jnp.broadcast_to(mine[None], (plane, 13, 2, BLOCK)), PLANE, PLANE_FIRST)
    whole = whole.reshape(plane, 26, BLOCK)
    devices = plane * depth
    grads, total = finish(
        whole.astype(jnp.float32),
        devices / WSCALE / grid_total,
        devices / LSCALE / (grid_total * V * members),
        width,
    )
    return (total[0, 0], grad_local[None], grads.T)


def solution(mesh):
    fine = Mesh(mesh.devices.reshape(2, 16, 2, 2, 4), GRID + MEMBER)
    in_specs = (P(MEMBER, GRID, None), P(), P(None, GRID), P(GRID))
    out_specs = (P(), P(MEMBER, GRID, None), P())
    return jax.shard_map(shards, mesh=fine, in_specs=in_specs, out_specs=out_specs, check_vma=False)
```

```python
import itertools

import jax
import jax.numpy as jnp
from jax import lax
from jax.experimental import pallas as pl
from jax.experimental.pallas import tpu as pltpu
from jax.sharding import Mesh, PartitionSpec as P

EPS_SQ = 0.0001
V = 100
BLOCK = 128
GROUPS = 4
MEMBER = ("y_hi", "x")
GRID = ("y_lo", "z", "core")
PLANE = ("y_hi", "y_lo", "x", "core")
MEMBER_FIRST = (1, 2)
PLANE_FIRST = (1, 1, 2, 1)
Z_FIRST = (8,)
WSCALE = 0.25
LSCALE = 1.0 / 512.0
VMEM = pl.BlockSpec(memory_space=pltpu.VMEM)
SMEM = pl.BlockSpec(memory_space=pltpu.SMEM)


def places(axes, first):
    sizes = [lax.axis_size(a) for a in axes]
    order = []
    for place in itertools.product(*map(range, sizes)):
        index = 0
        for step, begin, size in zip(place, first, sizes):
            index = index * size + (begin + step) % size
        order.append(index)
    return order


def exchange(x, axes, first):
    return lax.all_to_all(x, axes, 0, 0, axis_index_groups=[places(axes, first)], tiled=True)


def project_kernel(states, weight, goal, diff):
    for low in range(0, states.shape[0], 2 * BLOCK):
        both = lax.dot_general(
            weight[...],
            states[low : low + 2 * BLOCK, :],
            (((1,), (1,)), ((), ())),
            preferred_element_type=jnp.float32,
        )
        for part in range(2):
            r = low // BLOCK + part
            diff[r] = both[:V, part * BLOCK : (part + 1) * BLOCK] - goal[r]


def project(states, weight, goal):
    return pl.pallas_call(
        project_kernel,
        out_shape=jax.ShapeDtypeStruct(goal.shape, jnp.float32),
        in_specs=[VMEM, VMEM, VMEM],
        out_specs=VMEM,
        compiler_params=pltpu.CompilerParams(vmem_limit_bytes=8 * 1024 * 1024),
    )(states, weight, goal)


def pair_kernel(rank, diff, area, dpart, loss):
    members = diff.shape[0]
    coef = 1.0 / (members - 1)
    floor = coef * 0.5 * members * EPS_SQ**0.5
    weights = area[pl.ds(rank[0], 1), :]
    total = jnp.zeros((1, BLOCK), jnp.float32)
    for low in range(0, V, 16):
        high = min(low + 16, V)
        own = [diff[m, low:high, :] for m in range(members)]
        signs = [None] * members
        direct, size = None, None
        for m in range(members):
            square = own[m] * own[m] + EPS_SQ
            inv = lax.rsqrt(square)
            direct = square * inv if direct is None else direct + square * inv
            signs[m] = own[m] * inv
        pulls = [None] * members
        for i in range(members):
            for j in range(i + 1, members):
                delta = own[i] - own[j]
                square = delta * delta + EPS_SQ
                inv = lax.rsqrt(square)
                sign = delta * inv
                size = square * inv if size is None else size + square * inv
                pulls[i] = sign if pulls[i] is None else pulls[i] + sign
                pulls[j] = -sign if pulls[j] is None else pulls[j] - sign
        for m in range(members):
            dpart[m, low:high, :] = (weights * (signs[m] - coef * pulls[m])).astype(jnp.bfloat16)
        per = weights * (direct - coef * size - floor)
        total = total + jnp.sum(per, axis=0, keepdims=True)
    loss[...] = total


def pairs(rank, diff, area):
    return pl.pallas_call(
        pair_kernel,
        out_shape=(
            jax.ShapeDtypeStruct(diff.shape, jnp.bfloat16),
            jax.ShapeDtypeStruct((1, BLOCK), jnp.float32),
        ),
        in_specs=[SMEM, VMEM, VMEM],
        out_specs=(VMEM, VMEM),
        compiler_params=pltpu.CompilerParams(vmem_limit_bytes=8 * 1024 * 1024),
    )(rank, diff, area)


def finish_kernel(factor, loss_factor, table, grads, loss, ready, sems):
    columns = grads.shape[1] // BLOCK
    half = V // 2 // 16 * 16
    copies = [
        pltpu.make_async_copy(ready.at[:half], grads.at[:half], sems.at[0]),
        pltpu.make_async_copy(ready.at[half:], grads.at[half:], sems.at[1]),
    ]
    for g in range(GROUPS):
        for c in range(columns):
            piece = table[g * columns + c] * factor
            lanes = slice(c * BLOCK, (c + 1) * BLOCK)
            ready[24 * g : 24 * (g + 1), lanes] = piece[:24]
            ready[V - GROUPS + g : V - GROUPS + g + 1, lanes] = piece[24:25]
        if 24 * (g + 1) == half:
            copies[0].start()
    copies[1].start()
    lanes = table[0, 25:26, :] + table[1, 25:26, :] * (1.0 / 1024.0)
    loss[0, 0] = jnp.sum(lanes) * loss_factor
    copies[0].wait()
    copies[1].wait()


def finish(table, factor, loss_factor, width):
    return pl.pallas_call(
        lambda *refs: finish_kernel(factor, loss_factor, *refs),
        out_shape=(
            jax.ShapeDtypeStruct((V, width), jnp.float32),
            jax.ShapeDtypeStruct((1, 1), jnp.float32),
        ),
        in_specs=[VMEM],
        out_specs=(pl.BlockSpec(memory_space=pltpu.HBM), SMEM),
        scratch_shapes=[pltpu.VMEM((V, width), jnp.float32), pltpu.SemaphoreType.DMA((2,))],
        compiler_params=pltpu.CompilerParams(vmem_limit_bytes=8 * 1024 * 1024),
    )(table)


def shards(states, weight, target, area):
    members = lax.axis_size(MEMBER)
    plane = lax.axis_size(PLANE)
    depth = lax.axis_size("z")
    points, width = states.shape[1:]
    grid_total = points * lax.axis_size(GRID)
    rank = 0
    for axis, begin in zip(MEMBER, MEMBER_FIRST):
        size = lax.axis_size(axis)
        rank = rank * size + (lax.axis_index(axis) + size - begin) % size
    local_states = states[0]
    columns = width // BLOCK
    goal = lax.optimization_barrier(target.reshape(V, members, BLOCK).transpose(1, 0, 2))
    diff = project(local_states, jnp.pad(weight.T, ((0, 28), (0, 0))), goal)
    diff, rank = lax.optimization_barrier((diff.astype(jnp.float16), rank[None]))
    every = exchange(diff, MEMBER, MEMBER_FIRST).astype(jnp.float32)
    dpart, loss = pairs(rank, every, area.reshape(members, BLOCK))
    scaled = loss * LSCALE
    top = scaled.astype(jnp.float16)
    rest = ((scaled - top.astype(jnp.float32)) * 1024.0).astype(jnp.float16)
    spare = jnp.concatenate([top, rest])[None, None]
    spare = jnp.broadcast_to(spare, (GROUPS, columns // 2, 2, BLOCK))
    spare = spare.reshape(GROUPS, columns, 1, BLOCK)
    dpart, spare = lax.optimization_barrier((dpart, spare))
    dpred = exchange(dpart, MEMBER, MEMBER_FIRST).transpose(1, 0, 2).reshape(V, points)
    grad_local = lax.dot_general(
        dpred, weight, (((0,), (1,)), ((), ())), preferred_element_type=jnp.float32
    ).astype(jnp.bfloat16)
    wterm = lax.dot_general(
        dpred, local_states, (((1,), (0,)), ((), ())), preferred_element_type=jnp.float32
    )
    wterm = (wterm * WSCALE).astype(jnp.float16)
    body = wterm[: V - GROUPS].reshape(GROUPS, 24, columns, BLOCK).transpose(0, 2, 1, 3)
    last = wterm[V - GROUPS :].reshape(GROUPS, columns, 1, BLOCK)
    chunks = jnp.concatenate([body, last, spare], axis=2).reshape(plane, 13, 2, BLOCK)
    mine = jnp.sum(exchange(chunks, PLANE, PLANE_FIRST).astype(jnp.float32), axis=0)
    mine = (mine * (1.0 / plane)).astype(jnp.float16)
    ring = exchange(jnp.broadcast_to(mine[None], (depth, 13, 2, BLOCK)), ("z",), Z_FIRST)
    mine = jnp.sum(ring.astype(jnp.float32), axis=0)
    mine = (mine * (1.0 / depth)).astype(jnp.float16)
    whole = exchange(jnp.broadcast_to(mine[None], (plane, 13, 2, BLOCK)), PLANE, PLANE_FIRST)
    whole = whole.reshape(plane, 26, BLOCK)
    devices = plane * depth
    grads, total = finish(
        whole.astype(jnp.float32),
        devices / WSCALE / grid_total,
        devices / LSCALE / (grid_total * V * members),
        width,
    )
    return (total[0, 0], grad_local[None], grads.T)


def solution(mesh):
    fine = Mesh(mesh.devices.reshape(2, 16, 2, 2, 4), GRID + MEMBER)
    in_specs = (P(MEMBER, GRID, None), P(), P(None, GRID), P(GRID))
    out_specs = (P(), P(MEMBER, GRID, None), P())
    return jax.shard_map(shards, mesh=fine, in_specs=in_specs, out_specs=out_specs, check_vma=False)
```

```python
import itertools

import jax
import jax.numpy as jnp
from jax import lax
from jax.experimental import pallas as pl
from jax.experimental.pallas import tpu as pltpu
from jax.sharding import Mesh, PartitionSpec as P

EPS_SQ = 0.0001
V = 100
BLOCK = 128
GROUPS = 4
MEMBER = ("y_hi", "x")
GRID = ("y_lo", "z", "core")
PLANE = ("y_hi", "y_lo", "x", "core")
MEMBER_FIRST = (1, 2)
SUM_FIRST = (1, 1, 2, 1)
COPY_FIRST = (1, 0, 2, 1)
Z_FIRST = (8,)
WSCALE = 0.25
LSCALE = 1.0 / 512.0
VMEM = pl.BlockSpec(memory_space=pltpu.VMEM)
SMEM = pl.BlockSpec(memory_space=pltpu.SMEM)


def places(axes, first):
    sizes = [lax.axis_size(a) for a in axes]
    order = []
    for place in itertools.product(*map(range, sizes)):
        index = 0
        for step, begin, size in zip(place, first, sizes):
            index = index * size + (begin + step) % size
        order.append(index)
    return order


def exchange(x, axes, first):
    return lax.all_to_all(x, axes, 0, 0, axis_index_groups=[places(axes, first)], tiled=True)


def project_kernel(states, weight, goal, diff):
    for low in range(0, states.shape[0], 2 * BLOCK):
        both = lax.dot_general(
            weight[...],
            states[low : low + 2 * BLOCK, :],
            (((1,), (1,)), ((), ())),
            preferred_element_type=jnp.float32,
        )
        for part in range(2):
            r = low // BLOCK + part
            diff[r] = both[:V, part * BLOCK : (part + 1) * BLOCK] - goal[r]


def project(states, weight, goal):
    return pl.pallas_call(
        project_kernel,
        out_shape=jax.ShapeDtypeStruct(goal.shape, jnp.float32),
        in_specs=[VMEM, VMEM, VMEM],
        out_specs=VMEM,
        compiler_params=pltpu.CompilerParams(vmem_limit_bytes=8 * 1024 * 1024),
    )(states, weight, goal)


def pair_kernel(rank, diff, area, dpart, loss):
    members = diff.shape[0]
    coef = 1.0 / (members - 1)
    floor = coef * 0.5 * members * EPS_SQ**0.5
    weights = area[pl.ds(rank[0], 1), :]
    total = jnp.zeros((1, BLOCK), jnp.float32)
    for low in range(0, V, 16):
        high = min(low + 16, V)
        own = [diff[m, low:high, :] for m in range(members)]
        signs = [None] * members
        direct, size = None, None
        for m in range(members):
            square = own[m] * own[m] + EPS_SQ
            inv = lax.rsqrt(square)
            direct = square * inv if direct is None else direct + square * inv
            signs[m] = own[m] * inv
        pulls = [None] * members
        for i in range(members):
            for j in range(i + 1, members):
                delta = own[i] - own[j]
                square = delta * delta + EPS_SQ
                inv = lax.rsqrt(square)
                sign = delta * inv
                size = square * inv if size is None else size + square * inv
                pulls[i] = sign if pulls[i] is None else pulls[i] + sign
                pulls[j] = -sign if pulls[j] is None else pulls[j] - sign
        for m in range(members):
            dpart[m, low:high, :] = (weights * (signs[m] - coef * pulls[m])).astype(jnp.bfloat16)
        per = weights * (direct - coef * size - floor)
        total = total + jnp.sum(per, axis=0, keepdims=True)
    loss[...] = total


def pairs(rank, diff, area):
    return pl.pallas_call(
        pair_kernel,
        out_shape=(
            jax.ShapeDtypeStruct(diff.shape, jnp.bfloat16),
            jax.ShapeDtypeStruct((1, BLOCK), jnp.float32),
        ),
        in_specs=[SMEM, VMEM, VMEM],
        out_specs=(VMEM, VMEM),
        compiler_params=pltpu.CompilerParams(vmem_limit_bytes=8 * 1024 * 1024),
    )(rank, diff, area)


def finish_kernel(spots, factor, loss_factor, table, grads, loss):
    columns = grads.shape[1] // BLOCK
    for g in range(GROUPS):
        for c in range(columns):
            piece = table[spots[g * columns + c]] * factor
            lanes = slice(c * BLOCK, (c + 1) * BLOCK)
            grads[24 * g : 24 * (g + 1), lanes] = piece[:24]
            grads[V - GROUPS + g : V - GROUPS + g + 1, lanes] = piece[24:25]
    lanes = table[spots[0], 25:26, :] + table[spots[1], 25:26, :] * (1.0 / 1024.0)
    loss[0, 0] = jnp.sum(lanes) * loss_factor


def finish(table, spots, factor, loss_factor, width):
    return pl.pallas_call(
        lambda *refs: finish_kernel(spots, factor, loss_factor, *refs),
        out_shape=(
            jax.ShapeDtypeStruct((V, width), jnp.float32),
            jax.ShapeDtypeStruct((1, 1), jnp.float32),
        ),
        in_specs=[VMEM],
        out_specs=(pl.BlockSpec((V, width), lambda: (0, 0)), SMEM),
        compiler_params=pltpu.CompilerParams(vmem_limit_bytes=8 * 1024 * 1024),
    )(table)


def shards(states, weight, target, area):
    members = lax.axis_size(MEMBER)
    plane = lax.axis_size(PLANE)
    depth = lax.axis_size("z")
    points, width = states.shape[1:]
    grid_total = points * lax.axis_size(GRID)
    rank = 0
    for axis, begin in zip(MEMBER, MEMBER_FIRST):
        size = lax.axis_size(axis)
        rank = rank * size + (lax.axis_index(axis) + size - begin) % size
    local_states = states[0]
    columns = width // BLOCK
    goal = lax.optimization_barrier(target.reshape(V, members, BLOCK).transpose(1, 0, 2))
    diff = project(local_states, jnp.pad(weight.T, ((0, 28), (0, 0))), goal)
    diff, rank = lax.optimization_barrier((diff.astype(jnp.float16), rank[None]))
    every = exchange(diff, MEMBER, MEMBER_FIRST).astype(jnp.float32)
    dpart, loss = pairs(rank, every, area.reshape(members, BLOCK))
    scaled = loss * LSCALE
    top = scaled.astype(jnp.float16)
    rest = ((scaled - top.astype(jnp.float32)) * 1024.0).astype(jnp.float16)
    spare = jnp.concatenate([top, rest])[None, None]
    spare = jnp.broadcast_to(spare, (GROUPS, columns // 2, 2, BLOCK))
    spare = spare.reshape(GROUPS, columns, 1, BLOCK)
    dpart, spare = lax.optimization_barrier((dpart, spare))
    dpred = exchange(dpart, MEMBER, MEMBER_FIRST).transpose(1, 0, 2).reshape(V, points)
    grad_local = lax.dot_general(
        dpred, weight, (((0,), (1,)), ((), ())), preferred_element_type=jnp.float32
    ).astype(jnp.bfloat16)
    wterm = lax.dot_general(
        dpred, local_states, (((1,), (0,)), ((), ())), preferred_element_type=jnp.float32
    )
    wterm = (wterm * WSCALE).astype(jnp.float16)
    body = wterm[: V - GROUPS].reshape(GROUPS, 24, columns, BLOCK).transpose(0, 2, 1, 3)
    last = wterm[V - GROUPS :].reshape(GROUPS, columns, 1, BLOCK)
    chunks = jnp.concatenate([body, last, spare], axis=2).reshape(plane, 13, 2, BLOCK)
    mine = jnp.sum(exchange(chunks, PLANE, SUM_FIRST).astype(jnp.float32), axis=0)
    mine = (mine * (1.0 / plane)).astype(jnp.float16)
    ring = exchange(jnp.broadcast_to(mine[None], (depth, 13, 2, BLOCK)), ("z",), Z_FIRST)
    mine = jnp.sum(ring.astype(jnp.float32), axis=0)
    mine = (mine * (1.0 / depth)).astype(jnp.float16)
    whole = exchange(jnp.broadcast_to(mine[None], (plane, 13, 2, BLOCK)), PLANE, COPY_FIRST)
    whole = whole.reshape(plane, 26, BLOCK)
    devices = plane * depth
    copied = places(PLANE, COPY_FIRST)
    spots = [copied.index(device) for device in places(PLANE, SUM_FIRST)]
    grads, total = finish(
        whole.astype(jnp.float32),
        spots,
        devices / WSCALE / grid_total,
        devices / LSCALE / (grid_total * V * members),
        width,
    )
    return (total[0, 0], grad_local[None], grads.T)


def solution(mesh):
    fine = Mesh(mesh.devices.reshape(2, 16, 2, 2, 4), GRID + MEMBER)
    in_specs = (P(MEMBER, GRID, None), P(), P(None, GRID), P(GRID))
    out_specs = (P(), P(MEMBER, GRID, None), P())
    return jax.shard_map(shards, mesh=fine, in_specs=in_specs, out_specs=out_specs, check_vma=False)
```
